256 devices in a mesh: rep: 64 (over y_hi, z, x), fsdp: 4 (over y_lo, core).
Axes of the slice: x: 4, y: 4 (y_hi: 2, y_lo: 2; y = y_hi * 2 + y_lo), z: 8, core: 2. Of those that a mesh axis runs over, the one named last changes fastest.
Arguments:
- inputs: bfloat16 [64, 1024, 4096], P('rep', 'fsdp'), may hold values from -40 to 40
- cotangent: bfloat16 [64, 1024, 512], P('rep', 'fsdp'), may hold values from -6 to 6
- param: float32 [64, 4096, 512], P('rep', 'fsdp'), may hold values from -5 to 5
- momentum: float32 [64, 4096, 512], P('rep', 'fsdp'), may hold values from -3 to 3
- step: int32 [], replicated, may hold values from 0 to 999
Outputs:
- values: bfloat16 [64, 1024, 512], P('rep', 'fsdp')
- input_grad: bfloat16 [64, 1024, 4096], P('rep', 'fsdp')
- new_param: float32 [64, 4096, 512], P('rep', 'fsdp')
- new_momentum: float32 [64, 4096, 512], P('rep', 'fsdp')
The draws below stay inside these ranges and needn't reach their ends.
All inputs are finite; a program needn't handle non-finite values.
Results may differ from the reference program's by a relative error of at most 0.009.
Values may be sent and summed in bfloat16 or wider, within the bound.
A program may use at most 128 MiB of HBM per device.

```python
import math
import jax
import jax.numpy as jnp
from jax import lax

D = 4096
TOK_DEV = 256
E = 512
TOKENS = 1024
REPLICAS = 64
N_REP = 64
N_FSDP = 4


def draw_inputs(key, part):
    key = jax.random.fold_in(key, 11)
    first, second, third = jax.random.split(key, 3)
    base = jax.random.truncated_normal(first, -4.0, 4.0, (REPLICAS, TOKENS, D), jnp.float32)
    row_scale = jnp.exp(jax.random.uniform(second, (REPLICAS, TOKENS, 1), jnp.float32, math.log(0.3), math.log(3.0)))
    col_scale = jnp.exp(jax.random.uniform(third, (1, 1, D), jnp.float32, math.log(0.3), math.log(3.0)))
    return (base * row_scale * col_scale).astype(jnp.bfloat16)


def block_scale(rng, extent, cuts, low, high):
    loudness = 1.0
    for position, shards_of in cuts:
        steps = jax.random.uniform(jax.random.fold_in(jax.random.fold_in(rng, 6), position), (shards_of,), jnp.float32, low / len(cuts), high / len(cuts))
        loudness = loudness * jnp.repeat(jnp.exp(steps), extent[position] // shards_of).reshape((-1,) + (1,) * (len(extent) - 1 - position))
    return loudness


def centred(own_key, shape, spread, most, cuts=(), kind=jnp.bfloat16):
    level = block_scale(own_key, shape, cuts, -0.22, 0.18) if cuts else 1.0
    entries = jax.random.normal(own_key, shape, jnp.float32) * spread * level
    return jnp.minimum(jnp.maximum(entries, -most), most).astype(kind)


def setup_inputs(seed: int = 0) -> dict:
    key_of = jax.random.split(jax.random.key(seed), 6)
    return {
        "inputs": draw_inputs(jax.random.fold_in(key_of[5], 71), 0),
        "cotangent": centred(key_of[1], (REPLICAS, TOKENS, E), 1.0, 6.0, ((0, 64), (1, 4))),
        "param": centred(key_of[2], (REPLICAS, D, E), 1.0, 5.0, ((0, 64), (1, 4)), jnp.float32),
        "momentum": centred(key_of[3], (REPLICAS, D, E), 0.5, 3.0, ((0, 64), (1, 4)), jnp.float32),
        "step": jax.random.randint(key_of[4], (), 0, 1000).astype(jnp.int32),
    }


EPSILON = 1e-05
MOMENTUM_BETA = 0.9
LEARN_RATE = 0.1
WEIGHT_DECAY = 0.1

def replica_pass(tokens_in, upstream, weights, buffer_in):
    scale = D ** (-0.5)
    floats = tokens_in.astype(jnp.float32)
    inverse_rms = lax.rsqrt(lax.optimization_barrier(jnp.mean(floats * floats, axis=-1, keepdims=True)) + EPSILON)
    normed = (floats * inverse_rms).astype(jnp.bfloat16)
    weights_half = weights.astype(jnp.bfloat16)
    values = (scale * jnp.dot(normed, weights_half, preferred_element_type=jnp.float32)).astype(jnp.bfloat16)
    normed_grad = scale * jnp.dot(upstream, weights_half.T, preferred_element_type=jnp.float32)
    projection = lax.optimization_barrier(jnp.sum(normed_grad * floats, axis=-1, keepdims=True)) / D
    input_grad = (inverse_rms * normed_grad - inverse_rms ** 3 * floats * projection).astype(jnp.bfloat16)
    normed_blocks = normed.reshape(N_FSDP, TOK_DEV, D)
    upstream_blocks = upstream.reshape(N_FSDP, TOK_DEV, E)

    def block_term(blocks):
        return (scale * jnp.dot(blocks[0].T, blocks[1], preferred_element_type=jnp.float32)).astype(jnp.bfloat16)
    partials = lax.map(block_term, (normed_blocks, upstream_blocks))
    grad = lax.optimization_barrier(jnp.sum(partials.astype(jnp.float32), axis=0))
    mid_momentum = MOMENTUM_BETA * buffer_in + grad + WEIGHT_DECAY * weights
    mid_param = weights - LEARN_RATE * mid_momentum
    return (values, input_grad, mid_param, mid_momentum)

def reference(inputs, cotangent, param, momentum, step):

    def run_one(group):
        return replica_pass(group[0], group[1], group[2], group[3])
    values, input_grad, mid_param, mid_momentum = lax.map(run_one, (inputs, cotangent, param, momentum))
    levels = N_REP.bit_length() - 1
    distance = jnp.left_shift(jnp.int32(1), jnp.remainder(step, levels).astype(jnp.int32))
    partner = jnp.bitwise_xor(jnp.arange(N_REP, dtype=jnp.int32), distance)
    new_param = 0.5 * (mid_param + mid_param[partner])
    new_momentum = 0.5 * (mid_momentum + mid_momentum[partner])
    return (values, input_grad, new_param, new_momentum)
```

```python
import functools

import jax
import jax.numpy as jnp
from jax import lax
from jax.experimental import pallas as pl
from jax.experimental.pallas import tpu as pltpu
from jax.sharding import PartitionSpec as P

EPSILON = 1e-05
MOMENTUM_BETA = 0.9
LEARN_RATE = 0.1
WEIGHT_DECAY = 0.1

MESH = pl.DeviceIdType.MESH
F32 = jnp.float32
BF16 = jnp.bfloat16

CHUNK = 128
EARLY = 2


def dot(a, b, ca, cb):
    return lax.dot_general(a, b, (((ca,), (cb,)), ((), ())), preferred_element_type=F32)


def kernel(
    stride,
    x_hbm, c_hbm, p_hbm, m_hbm,
    val_hbm, ig_hbm, np_hbm, nm_hbm,
    xv, xs, cv, cs, css, pv, mv, w, gs, gr, rp, ms, rm, fwd, back, inv, vv, igv,
    in_p, in_x, in_c, in_m, out_v, out_ig, out_p, out_m,
    xs_s, xs_r, cs_s, cs_r, ya_s, ya_r, so_s, so_r, sf_s, sf_r,
    g_s, g_r, ep_s, ep_r, em_s, em_r,
):
    tokens, width = xv.shape
    rows, units = pv.shape
    scale = width ** (-0.5)
    n = rows // CHUNK

    rep = lax.axis_index("rep")
    f = lax.axis_index("fsdp")
    f1 = f + 1 - 2 * lax.rem(f, 2)
    f2 = f + 2 - 4 * lax.div(f, 2)
    f3 = f1 + 2 - 4 * lax.div(f, 2)
    partner = rep + stride * (1 - 2 * lax.rem(lax.div(rep, stride), 2))
    sib, across, peer = (rep, f1), (rep, f2), (partner, f)

    def part(k):
        return pl.ds(pl.multiple_of(k * CHUNK, CHUNK), CHUNK)

    def cols(owner, k):
        return pl.ds(pl.multiple_of(owner * rows + k * CHUNK, CHUNK), CHUNK)

    def block(owner):
        return pl.ds(pl.multiple_of(owner * rows, rows), rows)

    def remote(src, dst, send, recv, where):
        return pltpu.make_async_remote_copy(
            src_ref=src, dst_ref=dst, send_sem=send, recv_sem=recv,
            device_id=where, device_id_type=MESH,
        )

    def load_p(k):
        return pltpu.make_async_copy(p_hbm.at[part(k)], pv.at[part(k)], in_p.at[k])

    load_x = pltpu.make_async_copy(x_hbm, xv, in_x)
    load_c = pltpu.make_async_copy(c_hbm, cv, in_c)
    load_m = pltpu.make_async_copy(m_hbm, mv, in_m)

    def send_x(j, owner):
        return remote(x_hbm.at[:, block(owner)], xs.at[j], xs_s.at[j], xs_r.at[j], sib)

    send_c = remote(cs, css, cs_s, cs_r, sib)

    def gather_y(k):
        ref = w.at[f, part(k)]
        return remote(ref, ref, ya_s.at[k], ya_r.at[k], across)

    def gather_own(k):
        ref = w.at[f, part(k)]
        return remote(ref, ref, so_s.at[k], so_r.at[k], sib)

    def gather_fwd(k):
        ref = w.at[f2, part(k)]
        return remote(ref, ref, sf_s.at[k], sf_r.at[k], sib)

    def send_g(k):
        return remote(gs.at[part(k)], gr.at[part(k)], g_s.at[k], g_r.at[k], across)

    def swap_p(k):
        return remote(w.at[f, part(k)], rp.at[part(k)], ep_s.at[k], ep_r.at[k], peer)

    def swap_m(k):
        return remote(ms.at[part(k)], rm.at[part(k)], em_s.at[k], em_r.at[k], peer)

    def store_p(k):
        return pltpu.make_async_copy(pv.at[part(k)], np_hbm.at[part(k)], out_p.at[k])

    def store_m(k):
        return pltpu.make_async_copy(mv.at[part(k)], nm_hbm.at[part(k)], out_m.at[k])

    def loop(low, high, body):
        def step(k, carry):
            body(k)
            return carry
        lax.fori_loop(low, high, step, 0)

    barrier = pltpu.get_barrier_semaphore()
    for where in (sib, across, peer):
        pl.semaphore_signal(barrier, inc=1, device_id=where, device_id_type=MESH)
    loop(0, n, lambda k: load_p(k).start())
    load_x.start()
    load_c.start()
    load_m.start()
    pl.semaphore_wait(barrier, 3)

    def begin(k):
        load_p(k).wait()
        w[f, part(k)] = pv[part(k)].astype(BF16)
        swap_p(k).start()

        @pl.when(k < EARLY)
        def _():
            gather_y(k).start()

    loop(0, EARLY, begin)
    send_x(1, f3).start()
    send_x(0, f1).start()
    loop(EARLY, n, begin)
    loop(0, n, lambda k: gather_own(k).start())

    load_x.wait()
    load_c.wait()

    def square(j, total):
        part_x = xv[:, pl.ds(pl.multiple_of(j * 512, 512), 512)].astype(F32)
        return total + jnp.sum(part_x * part_x, axis=1, keepdims=True)

    total = lax.fori_loop(0, width // 512, square, jnp.zeros((tokens, 1), F32))
    inverse = lax.rsqrt(total / width + EPSILON)
    inv[...] = inverse
    cs[...] = (inverse * cv[...].astype(F32)).astype(BF16)
    send_c.start()

    def term(owner, j, k):
        mine = dot(xv[:, cols(owner, k)], cs[...], 0, 0)
        theirs = dot(xs[j, :, part(k)], css[...], 0, 0)
        return scale * (mine + theirs)

    send_x(1, f3).wait_recv()
    send_c.wait_recv()

    def give(k):
        gs[part(k)] = term(f2, 1, k).astype(BF16)
        send_g(k).start()

    loop(0, n, give)

    send_x(0, f1).wait_recv()
    load_m.wait()

    def keep(k):
        at = part(k)
        mv[at] = MOMENTUM_BETA * mv[at] + WEIGHT_DECAY * pv[at] + term(f, 0, k)

    loop(0, n, keep)

    def product(owner, k):
        piece = w[owner, part(k)]
        fwd[...] += dot(xv[:, cols(owner, k)], piece, 1, 0)
        back[:, cols(owner, k)] = dot(cv[...], piece, 1, 1)

    fwd[...] = jnp.zeros_like(fwd)

    def near(k):
        product(f, k)
        gather_own(k).wait_recv()
        product(f1, k)

    def pass_on(k):
        gather_y(k).wait_recv()
        gather_fwd(k).start()

    def far(k):
        product(f2, k)
        gather_fwd(k).wait_recv()
        product(f3, k)

    loop(0, EARLY, pass_on)
    loop(0, n, near)
    loop(0, EARLY, far)

    def fold(k):
        at = part(k)
        send_g(k).wait_recv()
        mid = mv[at] + gr[at].astype(F32)
        mv[at] = mid
        ms[at] = mid.astype(BF16)
        swap_m(k).start()

    def mix(k):
        at = part(k)
        swap_p(k).wait_recv()
        swap_m(k).wait_recv()
        momentum = 0.5 * (mv[at] + rm[at].astype(F32))
        mv[at] = momentum
        store_m(k).start()
        pv[at] = 0.5 * (pv[at] + rp[at].astype(F32)) - LEARN_RATE * momentum
        store_p(k).start()

    loop(0, n - 1, fold)
    loop(EARLY, n, lambda k: gather_y(k).start())
    fold(n - 1)

    def rest(k):
        pass_on(k)
        mix(k - EARLY)
        far(k)

    loop(EARLY, n, rest)

    inverse = inv[...]
    vv[...] = (scale * inverse * fwd[...]).astype(BF16)
    store_v = pltpu.make_async_copy(vv, val_hbm, out_v)
    store_v.start()
    projection = scale * jnp.sum(fwd[...] * cv[...].astype(F32), axis=1, keepdims=True) / width
    first = scale * inverse
    second = inverse**3 * projection

    def store_ig(j):
        at = pl.ds(pl.multiple_of(j * 512, 512), 512)
        return pltpu.make_async_copy(igv.at[:, at], ig_hbm.at[:, at], out_ig.at[j])

    def finish(j):
        at = pl.ds(pl.multiple_of(j * 512, 512), 512)
        igv[:, at] = (first * back[:, at] - second * xv[:, at].astype(F32)).astype(BF16)
        store_ig(j).start()

    loop(0, width // 512, finish)
    loop(n - EARLY, n, mix)

    store_v.wait()
    loop(0, width // 512, lambda j: store_ig(j).wait())
    send_x(0, f1).wait_send()
    send_x(1, f3).wait_send()
    send_c.wait_send()

    def drain(k):
        store_p(k).wait()
        store_m(k).wait()
        gather_y(k).wait_send()
        gather_own(k).wait_send()
        gather_fwd(k).wait_send()
        send_g(k).wait_send()
        swap_p(k).wait_send()
        swap_m(k).wait_send()

    loop(0, n, drain)


def run(level, x, c, p, m):
    tokens, width = x.shape
    rows, units = p.shape
    n = rows // CHUNK
    dma = pltpu.SemaphoreType.DMA
    anywhere = pl.BlockSpec(memory_space=pl.ANY)
    vmem = pltpu.VMEM
    return pl.pallas_call(
        functools.partial(kernel, 2**level),
        out_shape=(
            jax.ShapeDtypeStruct((tokens, units), BF16),
            jax.ShapeDtypeStruct((tokens, width), BF16),
            jax.ShapeDtypeStruct((rows, units), F32),
            jax.ShapeDtypeStruct((rows, units), F32),
        ),
        in_specs=[anywhere] * 4,
        out_specs=(anywhere,) * 4,
        scratch_shapes=[
            vmem((tokens, width), BF16),
            vmem((2, tokens, rows), BF16),
            vmem((tokens, units), BF16),
            vmem((tokens, units), BF16),
            vmem((tokens, units), BF16),
            vmem((rows, units), F32),
            vmem((rows, units), F32),
            vmem((4, rows, units), BF16),
            vmem((rows, units), BF16),
            vmem((rows, units), BF16),
            vmem((rows, units), BF16),
            vmem((rows, units), BF16),
            vmem((rows, units), BF16),
            vmem((tokens, units), F32),
            vmem((tokens, width), F32),
            vmem((tokens, 1), F32),
            vmem((tokens, units), BF16),
            vmem((tokens, width), BF16),
            dma((n,)), dma, dma, dma, dma, dma((width // 512,)), dma((n,)), dma((n,)),
            dma((2,)), dma((2,)), dma, dma,
            dma((n,)), dma((n,)), dma((n,)), dma((n,)), dma((n,)), dma((n,)),
            dma((n,)), dma((n,)), dma((n,)), dma((n,)), dma((n,)), dma((n,)),
        ],
        compiler_params=pltpu.CompilerParams(
            collective_id=level, has_side_effects=True, vmem_limit_bytes=48 * 2**20
        ),
        name="window" + str(level),
    )(x, c, p, m)


def on_device(inputs, cotangent, param, momentum, step):
    levels = lax.axis_size("rep").bit_length() - 1
    level = jnp.remainder(step, levels)
    outs = lax.switch(
        level,
        [functools.partial(run, position) for position in range(levels)],
        inputs[0], cotangent[0], param[0], momentum[0],
    )
    return tuple(out[None] for out in outs)


def solution(mesh):
    placed = P("rep", "fsdp", None)
    return jax.shard_map(
        on_device,
        mesh=mesh,
        in_specs=(placed, placed, placed, placed, P()),
        out_specs=(placed,) * 4,
        check_vma=False,
    )
```

```python
import functools

import jax
import jax.numpy as jnp
from jax import lax
from jax.experimental import pallas as pl
from jax.experimental.pallas import tpu as pltpu
from jax.sharding import PartitionSpec as P

EPSILON = 1e-05
MOMENTUM_BETA = 0.9
LEARN_RATE = 0.1
WEIGHT_DECAY = 0.1

MESH = pl.DeviceIdType.MESH
F32 = jnp.float32
BF16 = jnp.bfloat16

CHUNK = 128
PIECES = 4


def dot(a, b, ca, cb):
    return lax.dot_general(a, b, (((ca,), (cb,)), ((), ())), preferred_element_type=F32)


def kernel(
    stride, early, relay,
    x_hbm, c_hbm, p_hbm, m_hbm,
    vv, xv, back, factors, pv, rp, mv, rm,
    xs, cv, cs, css, w, gs, gr, ms, fwd, inv,
    in_p, in_x, in_c, in_m,
    xs_s, xs_r, cs_s, cs_r, ya_s, ya_r, so_s, so_r, sf_s, sf_r,
    g_s, g_r, ep_s, ep_r, em_s, em_r,
):
    tokens, width = xv.shape
    rows, units = pv.shape
    scale = width ** (-0.5)
    n = rows // CHUNK

    rep = lax.axis_index("rep")
    f = lax.axis_index("fsdp")
    f1 = f + 1 - 2 * lax.rem(f, 2)
    f2 = f + 2 - 4 * lax.div(f, 2)
    f3 = f1 + 2 - 4 * lax.div(f, 2)
    partner = rep + stride * (1 - 2 * lax.rem(lax.div(rep, stride), 2))
    sib, across, peer, beyond = (rep, f1), (rep, f2), (partner, f), (partner, f2)

    def part(k):
        return pl.ds(pl.multiple_of(k * CHUNK, CHUNK), CHUNK)

    def cols(owner, k):
        return pl.ds(pl.multiple_of(owner * rows + k * CHUNK, CHUNK), CHUNK)

    def block(owner):
        return pl.ds(pl.multiple_of(owner * rows, rows), rows)

    def remote(src, dst, send, recv, where):
        return pltpu.make_async_remote_copy(
            src_ref=src, dst_ref=dst, send_sem=send, recv_sem=recv,
            device_id=where, device_id_type=MESH,
        )

    def load_p(k):
        return pltpu.make_async_copy(p_hbm.at[part(k)], pv.at[part(k)], in_p.at[k])

    load_x = pltpu.make_async_copy(x_hbm, xv, in_x)
    load_c = pltpu.make_async_copy(c_hbm, cv, in_c)
    load_m = pltpu.make_async_copy(m_hbm, mv, in_m)

    def send_x(j, owner):
        return remote(x_hbm.at[:, block(owner)], xs.at[j], xs_s.at[j], xs_r.at[j], sib)

    send_c = remote(cs, css, cs_s, cs_r, sib)

    def gather_y(k):
        ref = w.at[f, part(k)]
        return remote(ref, ref, ya_s.at[k], ya_r.at[k], across)

    def gather_own(k):
        ref = w.at[f, part(k)]
        return remote(ref, ref, so_s.at[k], so_r.at[k], sib)

    def gather_fwd(k):
        ref = w.at[f2, part(k)]
        return remote(ref, ref, sf_s.at[k], sf_r.at[k], sib)

    def send_g(k):
        where = (rep + lax.rem(k, 2) * (partner - rep), f2) if relay else across
        return remote(gs.at[part(k)], gr.at[part(k)], g_s.at[k], g_r.at[k], where)

    def swap_p(k):
        owner, where = (f2, beyond) if relay else (f, peer)
        return remote(w.at[owner, part(k)], rp.at[part(k)], ep_s.at[k], ep_r.at[k], where)

    def swap_m(k):
        return remote(ms.at[part(k)], rm.at[part(k)], em_s.at[k], em_r.at[k], peer)

    def loop(low, high, body):
        def step(k, carry):
            body(k)
            return carry
        lax.fori_loop(low, high, step, 0)

    barrier = pltpu.get_barrier_semaphore()
    friends = (sib, across, peer, beyond) if relay else (sib, across, peer)
    for where in friends:
        pl.semaphore_signal(barrier, inc=1, device_id=where, device_id_type=MESH)
    loop(0, n, lambda k: load_p(k).start())
    load_x.start()
    load_c.start()
    load_m.start()
    pl.semaphore_wait(barrier, len(friends))

    def begin(k):
        load_p(k).wait()
        w[f, part(k)] = pv[part(k)].astype(BF16)
        if not relay:
            swap_p(k).start()

        @pl.when(k < early)
        def _():
            gather_y(k).start()

    loop(0, early, begin)
    send_x(1, f3).start()
    send_x(0, f1).start()
    loop(early, n, begin)
    loop(0, n, lambda k: gather_own(k).start())

    load_x.wait()
    load_c.wait()

    def square(j, total):
        part_x = xv[:, pl.ds(pl.multiple_of(j * 512, 512), 512)].astype(F32)
        return total + jnp.sum(part_x * part_x, axis=1, keepdims=True)

    total = lax.fori_loop(0, width // 512, square, jnp.zeros((tokens, 1), F32))
    inverse = lax.rsqrt(total / width + EPSILON)
    inv[...] = inverse
    cs[...] = (inverse * cv[...].astype(F32)).astype(BF16)
    send_c.start()

    def term(owner, j, k):
        mine = dot(xv[:, cols(owner, k)], cs[...], 0, 0)
        theirs = dot(xs[j, :, part(k)], css[...], 0, 0)
        return scale * (mine + theirs)

    send_x(1, f3).wait_recv()
    send_c.wait_recv()

    def give(k):
        gs[part(k)] = term(f2, 1, k).astype(BF16)
        send_g(k).start()

    loop(0, n, give)

    send_x(0, f1).wait_recv()
    load_m.wait()

    def keep(k):
        at = part(k)
        mv[at] = MOMENTUM_BETA * mv[at] + WEIGHT_DECAY * pv[at] + term(f, 0, k)

    loop(0, n, keep)

    def product(owner, k):
        piece = w[owner, part(k)]
        fwd[...] += dot(xv[:, cols(owner, k)], piece, 1, 0)
        back[:, cols(owner, k)] = dot(cv[...], piece, 1, 1)

    fwd[...] = jnp.zeros_like(fwd)

    def near(k):
        product(f, k)
        gather_own(k).wait_recv()
        product(f1, k)

    def pass_on(k):
        gather_y(k).wait_recv()
        gather_fwd(k).start()
        if relay:
            swap_p(k).start()

    def far(k):
        product(f2, k)
        gather_fwd(k).wait_recv()
        product(f3, k)

    loop(0, early, pass_on)
    loop(0, n, near)
    loop(0, early, far)

    def fold(k):
        at = part(k)
        send_g(k).wait_recv()
        mid = mv[at] + gr[at].astype(F32)
        mv[at] = mid
        ms[at] = mid.astype(BF16)
        swap_m(k).start()

    loop(0, n - 1, fold)
    loop(early, n, lambda k: gather_y(k).start())
    fold(n - 1)

    def rest(k):
        pass_on(k)
        far(k)

    loop(early, n, rest)

    inverse = inv[...]
    vv[...] = (scale * inverse * fwd[...]).astype(BF16)
    projection = scale * jnp.sum(fwd[...] * cv[...].astype(F32), axis=1, keepdims=True) / width
    factors[0] = scale * inverse
    factors[1] = inverse**3 * projection

    send_x(0, f1).wait_send()
    send_x(1, f3).wait_send()
    send_c.wait_send()

    def drain(k):
        swap_p(k).wait_recv()
        swap_m(k).wait_recv()
        gather_y(k).wait_send()
        gather_own(k).wait_send()
        gather_fwd(k).wait_send()
        send_g(k).wait_send()
        swap_p(k).wait_send()
        swap_m(k).wait_send()

    loop(0, n, drain)


def place(values, xv, back, factors, pv, rp, mv, rm, vo, igo, po, mo, ig, new_p, new_m, done):
    copies = []

    def leave(source, target):
        copy = pltpu.make_async_copy(source, target, done.at[len(copies)])
        copy.start()
        copies.append(copy)

    leave(values, vo)
    size = xv.shape[0] // PIECES
    for j in range(PIECES):
        at = pl.ds(j * size, size)
        ig[at] = (factors[0, at] * back[at] - factors[1, at] * xv[at].astype(F32)).astype(BF16)
        leave(ig.at[at], igo.at[at])
    size = pv.shape[0] // PIECES
    for j in range(PIECES):
        at = pl.ds(j * size, size)
        momentum = 0.5 * (mv[at] + rm[at].astype(F32))
        new_m[at] = momentum
        leave(new_m.at[at], mo.at[at])
        new_p[at] = 0.5 * (pv[at] + rp[at].astype(F32)) - LEARN_RATE * momentum
        leave(new_p.at[at], po.at[at])
    for copy in copies:
        copy.wait()


def settle(*arrays):
    values, xv, back, factors, pv, rp, mv, rm = arrays
    results = (values, xv, pv, mv)
    return pl.pallas_call(
        place,
        out_shape=tuple(jax.ShapeDtypeStruct(a.shape, a.dtype) for a in results),
        in_specs=[pl.BlockSpec(memory_space=pltpu.VMEM)] * 8,
        out_specs=(pl.BlockSpec(memory_space=pl.ANY),) * 4,
        scratch_shapes=[
            pltpu.VMEM(xv.shape, BF16),
            pltpu.VMEM(pv.shape, F32),
            pltpu.VMEM(mv.shape, F32),
            pltpu.SemaphoreType.DMA((1 + 3 * PIECES,)),
        ],
        compiler_params=pltpu.CompilerParams(vmem_limit_bytes=28 * 2**20),
        name="settle",
    )(*arrays)


def run(level, levels, x, c, p, m):
    tokens, width = x.shape
    rows, units = p.shape
    n = rows // CHUNK
    relay = level == levels - 1
    early = n // 2 if relay else n // 4
    dma = pltpu.SemaphoreType.DMA
    vmem = pltpu.VMEM
    shape = jax.ShapeDtypeStruct
    outs = pl.pallas_call(
        functools.partial(kernel, 2**level, early, relay),
        out_shape=(
            shape((tokens, units), BF16),
            shape((tokens, width), BF16),
            shape((tokens, width), F32),
            shape((2, tokens, 1), F32),
            shape((rows, units), F32),
            shape((rows, units), BF16),
            shape((rows, units), F32),
            shape((rows, units), BF16),
        ),
        in_specs=[pl.BlockSpec(memory_space=pl.ANY)] * 4,
        out_specs=(pl.BlockSpec(memory_space=vmem),) * 8,
        scratch_shapes=[
            vmem((2, tokens, rows), BF16),
            vmem((tokens, units), BF16),
            vmem((tokens, units), BF16),
            vmem((tokens, units), BF16),
            vmem((4, rows, units), BF16),
            vmem((rows, units), BF16),
            vmem((rows, units), BF16),
            vmem((rows, units), BF16),
            vmem((tokens, units), F32),
            vmem((tokens, 1), F32),
            dma((n,)), dma, dma, dma,
            dma((2,)), dma((2,)), dma, dma,
            dma((n,)), dma((n,)), dma((n,)), dma((n,)), dma((n,)), dma((n,)),
            dma((n,)), dma((n,)), dma((n,)), dma((n,)), dma((n,)), dma((n,)),
        ],
        compiler_params=pltpu.CompilerParams(
            collective_id=level, has_side_effects=True, vmem_limit_bytes=30 * 2**20
        ),
        name="window" + str(level),
    )(x, c, p, m)
    return settle(*outs)


def on_device(inputs, cotangent, param, momentum, step):
    levels = lax.axis_size("rep").bit_length() - 1
    level = jnp.remainder(step, levels)
    outs = lax.switch(
        level,
        [functools.partial(run, position, levels) for position in range(levels)],
        inputs[0], cotangent[0], param[0], momentum[0],
    )
    return tuple(out[None] for out in outs)


def solution(mesh):
    placed = P("rep", "fsdp", None)
    return jax.shard_map(
        on_device,
        mesh=mesh,
        in_specs=(placed, placed, placed, placed, P()),
        out_specs=(placed,) * 4,
        check_vma=False,
    )
```

```python
import functools

import jax
import jax.numpy as jnp
from jax import lax
from jax.experimental import pallas as pl
from jax.experimental.pallas import tpu as pltpu
from jax.sharding import PartitionSpec as P

EPSILON = 1e-05
MOMENTUM_BETA = 0.9
LEARN_RATE = 0.1
WEIGHT_DECAY = 0.1

MESH = pl.DeviceIdType.MESH
F32 = jnp.float32
BF16 = jnp.bfloat16

CHUNK = 128
PIECES = 8


def dot(a, b, ca, cb):
    return lax.dot_general(a, b, (((ca,), (cb,)), ((), ())), preferred_element_type=F32)


def kernel(
    stride, early, depth, relay,
    x_hbm, c_hbm, p_hbm, m_hbm,
    cv, xv, fwd, back, inv, pv, rp, mv, rm,
    xs, cs, css, w, gs, gr, ms,
    in_p, in_x, in_c, in_m,
    xs_s, xs_r, cs_s, cs_r, ya_s, ya_r, so_s, so_r, sf_s, sf_r,
    g_s, g_r, ep_s, ep_r, em_s, em_r,
):
    tokens, width = xv.shape
    rows, units = pv.shape
    scale = width ** (-0.5)
    n = rows // CHUNK

    rep = lax.axis_index("rep")
    f = lax.axis_index("fsdp")
    f1 = f + 1 - 2 * lax.rem(f, 2)
    f2 = f + 2 - 4 * lax.div(f, 2)
    f3 = f1 + 2 - 4 * lax.div(f, 2)
    partner = rep + stride * (1 - 2 * lax.rem(lax.div(rep, stride), 2))
    sib, across, peer, beyond = (rep, f1), (rep, f2), (partner, f), (partner, f2)

    def part(k):
        return pl.ds(pl.multiple_of(k * CHUNK, CHUNK), CHUNK)

    def cols(owner, k):
        return pl.ds(pl.multiple_of(owner * rows + k * CHUNK, CHUNK), CHUNK)

    def block(owner):
        return pl.ds(pl.multiple_of(owner * rows, rows), rows)

    def remote(src, dst, send, recv, where):
        return pltpu.make_async_remote_copy(
            src_ref=src, dst_ref=dst, send_sem=send, recv_sem=recv,
            device_id=where, device_id_type=MESH,
        )

    def load_p(k):
        return pltpu.make_async_copy(p_hbm.at[part(k)], pv.at[part(k)], in_p.at[k])

    load_x = pltpu.make_async_copy(x_hbm, xv, in_x)
    load_c = pltpu.make_async_copy(c_hbm, cv, in_c)
    load_m = pltpu.make_async_copy(m_hbm, mv, in_m)

    def send_x(j, owner):
        return remote(xv.at[:, block(owner)], xs.at[j], xs_s.at[j], xs_r.at[j], sib)

    send_c = remote(cs, css, cs_s, cs_r, sib)

    def gather_y(k):
        ref = w.at[f, part(k)]
        return remote(ref, ref, ya_s.at[k], ya_r.at[k], across)

    def gather_own(k):
        ref = w.at[f, part(k)]
        return remote(ref, ref, so_s.at[k], so_r.at[k], sib)

    def gather_fwd(k):
        ref = w.at[f2, part(k)]
        return remote(ref, ref, sf_s.at[k], sf_r.at[k], sib)

    def send_g(k):
        where = (rep + lax.rem(k, 2) * (partner - rep), f2) if relay else across
        return remote(gs.at[part(k)], gr.at[part(k)], g_s.at[k], g_r.at[k], where)

    def swap_p(k):
        owner, where = (f2, beyond) if relay else (f, peer)
        return remote(w.at[owner, part(k)], rp.at[part(k)], ep_s.at[k], ep_r.at[k], where)

    def swap_m(k):
        return remote(ms.at[part(k)], rm.at[part(k)], em_s.at[k], em_r.at[k], peer)

    def loop(low, high, body):
        def step(k, carry):
            body(k)
            return carry
        lax.fori_loop(low, high, step, 0)

    barrier = pltpu.get_barrier_semaphore()
    friends = (sib, across, peer, beyond) if relay else (sib, across, peer)
    for where in friends:
        pl.semaphore_signal(barrier, inc=1, device_id=where, device_id_type=MESH)
    loop(0, n, lambda k: load_p(k).start())
    load_x.start()
    load_c.start()
    load_m.start()

    def begin(k):
        if not relay:
            swap_p(k).start()

    def shorten(k):
        load_p(k).wait()
        w[f, part(k)] = pv[part(k)].astype(BF16)

    loop(0, early, shorten)
    pl.semaphore_wait(barrier, len(friends))

    def open_up(k):
        begin(k)
        gather_y(k).start()

    def follow(k):
        shorten(k)
        begin(k)

    loop(0, early, open_up)
    loop(early, n, follow)
    loop(0, n, lambda k: gather_own(k).start())

    load_x.wait()
    send_x(1, f3).start()
    send_x(0, f1).start()
    load_c.wait()

    def add_square(j, total):
        part_x = xv[:, pl.ds(pl.multiple_of(j * 512, 512), 512)].astype(F32)
        return total + jnp.sum(part_x * part_x, axis=1, keepdims=True)

    total = lax.fori_loop(0, width // 512, add_square, jnp.zeros((tokens, 1), F32))
    inverse = lax.rsqrt(total / width + EPSILON)
    inv[...] = inverse
    cs[...] = (inverse * cv[...].astype(F32)).astype(BF16)
    send_c.start()

    def term(owner, j, k):
        mine = dot(xv[:, cols(owner, k)], cs[...], 0, 0)
        theirs = dot(xs[j, :, part(k)], css[...], 0, 0)
        return scale * (mine + theirs)

    def keep(k):
        at = part(k)
        mv[at] = MOMENTUM_BETA * mv[at] + WEIGHT_DECAY * pv[at] + term(f, 0, k)

    def product(owner, k):
        piece = w[owner, part(k)]
        fwd[...] += dot(xv[:, cols(owner, k)], piece, 1, 0)
        back[:, cols(owner, k)] = dot(cv[...], piece, 1, 1)

    fwd[...] = jnp.zeros_like(fwd)

    def near(k):
        product(f, k)
        gather_own(k).wait_recv()
        product(f1, k)

    def pass_on(k):
        gather_y(k).wait_recv()
        gather_fwd(k).start()
        if relay:
            swap_p(k).start()

    def far(k):
        product(f2, k)
        gather_fwd(k).wait_recv()
        product(f3, k)

    def fold(k):
        at = part(k)
        send_g(k).wait_recv()
        mid = mv[at] + gr[at].astype(F32)
        mv[at] = mid
        ms[at] = mid.astype(BF16)
        swap_m(k).start()

    send_x(1, f3).wait_recv()
    send_c.wait_recv()
    send_x(0, f1).wait_recv()
    load_m.wait()

    def reduce_step(k):
        gs[part(k)] = term(f2, 1, k).astype(BF16)

        @pl.when(k < depth)
        def _():
            gather_y(early - depth + k).wait_send()

        @pl.when(k >= depth)
        def _():
            send_g(k - depth).wait_send()

        send_g(k).start()

        @pl.when(k < early)
        def _():
            pass_on(k)

        keep(k)
        near(k)

        @pl.when((k >= 1) & (k <= early))
        def _():
            far(k - 1)

        @pl.when(k >= depth)
        def _():
            fold(k - depth)

    loop(0, n, reduce_step)

    def gather_step(k):
        j = k - early

        @pl.when(j < depth)
        def _():
            send_g(n - depth + j).wait_send()

        @pl.when((j >= depth) & (k < n))
        def _():
            gather_y(k - depth).wait_send()

        @pl.when(k < n)
        def _():
            gather_y(k).start()

        @pl.when(j < depth)
        def _():
            fold(n - depth + j)

        @pl.when((j >= 2) & (k < n + 2))
        def _():
            pass_on(k - 2)

        @pl.when(j >= 3)
        def _():
            far(k - 3)

    def drain_first(k):
        gather_own(k).wait_send()
        swap_p(k).wait_recv()
        swap_p(k).wait_send()

    def drain_last(k):
        gather_fwd(k).wait_send()
        swap_m(k).wait()

    loop(early, n + 1, gather_step)
    send_x(0, f1).wait_send()
    send_x(1, f3).wait_send()
    send_c.wait_send()
    if not relay:
        loop(0, n, drain_first)
    loop(n + 1, n + 3, gather_step)
    if relay:
        loop(0, n, drain_first)
    loop(n - depth, n, lambda k: gather_y(k).wait_send())
    loop(0, n, drain_last)


def place(
    cv, xv, fwd, back, inv, pv, rp, mv, rm, vo, igo, po, mo, values, ig, new_p, new_m, done
):
    copies = []

    def leave(source, target):
        copy = pltpu.make_async_copy(source, target, done.at[len(copies)])
        copy.start()
        copies.append(copy)

    size = pv.shape[0] // PIECES
    for j in range(PIECES):
        at = pl.ds(j * size, size)
        momentum = 0.5 * (mv[at] + rm[at].astype(F32))
        new_m[at] = momentum
        leave(new_m.at[at], mo.at[at])
        new_p[at] = 0.5 * (pv[at] + rp[at].astype(F32)) - LEARN_RATE * momentum
        leave(new_p.at[at], po.at[at])
    tokens, width = xv.shape
    scale = width ** (-0.5)
    inverse = inv[...]
    values[...] = (scale * inverse * fwd[...]).astype(BF16)
    leave(values, vo)
    projection = scale * jnp.sum(fwd[...] * cv[...].astype(F32), axis=1, keepdims=True) / width
    first = scale * inverse
    second = inverse**3 * projection
    size = tokens // PIECES
    for j in range(PIECES):
        at = pl.ds(j * size, size)
        rows = slice(j * size, (j + 1) * size)
        ig[at] = (first[rows] * back[at] - second[rows] * xv[at].astype(F32)).astype(BF16)
        leave(ig.at[at], igo.at[at])
    for copy in copies:
        copy.wait()


def settle(*arrays):
    cv, xv, fwd, back, inv, pv, rp, mv, rm = arrays
    results = (cv, xv, pv, mv)
    return pl.pallas_call(
        place,
        out_shape=tuple(jax.ShapeDtypeStruct(a.shape, a.dtype) for a in results),
        in_specs=[pl.BlockSpec(memory_space=pltpu.VMEM)] * 9,
        out_specs=(pl.BlockSpec(memory_space=pl.ANY),) * 4,
        scratch_shapes=[
            pltpu.VMEM(cv.shape, BF16),
            pltpu.VMEM(xv.shape, BF16),
            pltpu.VMEM(pv.shape, F32),
            pltpu.VMEM(mv.shape, F32),
            pltpu.SemaphoreType.DMA((1 + 3 * PIECES,)),
        ],
        compiler_params=pltpu.CompilerParams(vmem_limit_bytes=28 * 2**20),
        name="settle",
    )(*arrays)


def run(level, levels, x, c, p, m):
    tokens, width = x.shape
    rows, units = p.shape
    n = rows // CHUNK
    relay = level == levels - 1
    early, depth = (n // 2, n // 2) if relay else (n // 4, n // 4)
    dma = pltpu.SemaphoreType.DMA
    vmem = pltpu.VMEM
    shape = jax.ShapeDtypeStruct
    outs = pl.pallas_call(
        functools.partial(kernel, 2**level, early, depth, relay),
        out_shape=(
            shape((tokens, units), BF16),
            shape((tokens, width), BF16),
            shape((tokens, units), F32),
            shape((tokens, width), F32),
            shape((tokens, 1), F32),
            shape((rows, units), F32),
            shape((rows, units), BF16),
            shape((rows, units), F32),
            shape((rows, units), BF16),
        ),
        in_specs=[pl.BlockSpec(memory_space=pl.ANY)] * 4,
        out_specs=(pl.BlockSpec(memory_space=vmem),) * 9,
        scratch_shapes=[
            vmem((2, tokens, rows), BF16),
            vmem((tokens, units), BF16),
            vmem((tokens, units), BF16),
            vmem((4, rows, units), BF16),
            vmem((rows, units), BF16),
            vmem((rows, units), BF16),
            vmem((rows, units), BF16),
            dma((n,)), dma, dma, dma,
            dma((2,)), dma((2,)), dma, dma,
            dma((n,)), dma((n,)), dma((n,)), dma((n,)), dma((n,)), dma((n,)),
            dma((n,)), dma((n,)), dma((n,)), dma((n,)), dma((n,)), dma((n,)),
        ],
        compiler_params=pltpu.CompilerParams(
            collective_id=level, has_side_effects=True, vmem_limit_bytes=30 * 2**20
        ),
        name="window" + str(level),
    )(x, c, p, m)
    return settle(*outs)


def on_device(inputs, cotangent, param, momentum, step):
    levels = lax.axis_size("rep").bit_length() - 1
    level = jnp.remainder(step, levels)
    outs = lax.switch(
        level,
        [functools.partial(run, position, levels) for position in range(levels)],
        inputs[0], cotangent[0], param[0], momentum[0],
    )
    return tuple(out[None] for out in outs)


def solution(mesh):
    placed = P("rep", "fsdp", None)
    return jax.shard_map(
        on_device,
        mesh=mesh,
        in_specs=(placed, placed, placed, placed, P()),
        out_specs=(placed,) * 4,
        check_vma=False,
    )
```

```python
import functools

import jax
import jax.numpy as jnp
from jax import lax
from jax.experimental import pallas as pl
from jax.experimental.pallas import tpu as pltpu
from jax.sharding import PartitionSpec as P

EPSILON = 1e-05
MOMENTUM_BETA = 0.9
LEARN_RATE = 0.1
WEIGHT_DECAY = 0.1

MESH = pl.DeviceIdType.MESH
F32 = jnp.float32
BF16 = jnp.bfloat16

CHUNK = 128
PIECES = 8


def dot(a, b, ca, cb):
    return lax.dot_general(a, b, (((ca,), (cb,)), ((), ())), preferred_element_type=F32)


def kernel(
    stride, early, depth, relay,
    x_hbm, c_hbm, p_hbm, m_hbm,
    cv, xv, fwd, back, inv, pv, rp, mv, rm,
    xs, cs, css, w, gs, gr, ms,
    in_p, in_x, in_c, in_m,
    xs_s, xs_r, cs_s, cs_r, ya_s, ya_r, so_s, so_r, sf_s, sf_r,
    g_s, g_r, ep_s, ep_r, em_s, em_r,
):
    tokens, width = xv.shape
    rows, units = pv.shape
    scale = width ** (-0.5)
    n = rows // CHUNK

    rep = lax.axis_index("rep")
    f = lax.axis_index("fsdp")
    f1 = f + 1 - 2 * lax.rem(f, 2)
    f2 = f + 2 - 4 * lax.div(f, 2)
    f3 = f1 + 2 - 4 * lax.div(f, 2)
    partner = rep + stride * (1 - 2 * lax.rem(lax.div(rep, stride), 2))
    sib, across, peer, beyond = (rep, f1), (rep, f2), (partner, f), (partner, f2)

    def part(k):
        return pl.ds(pl.multiple_of(k * CHUNK, CHUNK), CHUNK)

    def cols(owner, k):
        return pl.ds(pl.multiple_of(owner * rows + k * CHUNK, CHUNK), CHUNK)

    def block(owner):
        return pl.ds(pl.multiple_of(owner * rows, rows), rows)

    def remote(src, dst, send, recv, where):
        return pltpu.make_async_remote_copy(
            src_ref=src, dst_ref=dst, send_sem=send, recv_sem=recv,
            device_id=where, device_id_type=MESH,
        )

    def load_p(k):
        return pltpu.make_async_copy(p_hbm.at[part(k)], pv.at[part(k)], in_p.at[k])

    load_x = pltpu.make_async_copy(x_hbm, xv, in_x)
    load_c = pltpu.make_async_copy(c_hbm, cv, in_c)
    load_m = pltpu.make_async_copy(m_hbm, mv, in_m)

    def send_x(j, owner):
        return remote(xv.at[:, block(owner)], xs.at[j], xs_s.at[j], xs_r.at[j], sib)

    send_c = remote(cs, css, cs_s, cs_r, sib)

    def gather_y(k):
        ref = w.at[f, part(k)]
        return remote(ref, ref, ya_s.at[k], ya_r.at[k], across)

    def gather_own(k):
        ref = w.at[f, part(k)]
        return remote(ref, ref, so_s.at[k], so_r.at[k], sib)

    def gather_fwd(k):
        ref = w.at[f2, part(k)]
        return remote(ref, ref, sf_s.at[k], sf_r.at[k], sib)

    def send_g(k):
        where = (rep + lax.rem(k, 2) * (partner - rep), f2) if relay else across
        return remote(gs.at[part(k)], gr.at[part(k)], g_s.at[k], g_r.at[k], where)

    def swap_p(k):
        owner, where = (f2, beyond) if relay else (f, peer)
        return remote(w.at[owner, part(k)], rp.at[part(k)], ep_s.at[k], ep_r.at[k], where)

    def swap_m(k):
        return remote(ms.at[part(k)], rm.at[part(k)], em_s.at[k], em_r.at[k], peer)

    def loop(low, high, body):
        def step(k, carry):
            body(k)
            return carry
        lax.fori_loop(low, high, step, 0)

    barrier = pltpu.get_barrier_semaphore()
    friends = (sib, across, peer, beyond) if relay else (sib, across, peer)
    for where in friends:
        pl.semaphore_signal(barrier, inc=1, device_id=where, device_id_type=MESH)
    loop(0, n, lambda k: load_p(k).start())
    load_x.start()
    load_c.start()
    load_m.start()

    def begin(k):
        if not relay:
            swap_p(k).start()

    def shorten(k):
        load_p(k).wait()
        w[f, part(k)] = pv[part(k)].astype(BF16)

    loop(0, early, shorten)
    pl.semaphore_wait(barrier, len(friends))

    def open_up(k):
        begin(k)
        gather_y(k).start()

    def follow(k):
        shorten(k)
        begin(k)

    loop(0, early, open_up)
    loop(early, n, follow)
    loop(0, n, lambda k: gather_own(k).start())

    load_x.wait()
    send_x(1, f3).start()
    send_x(0, f1).start()
    load_c.wait()

    def add_square(j, total):
        part_x = xv[:, pl.ds(pl.multiple_of(j * 512, 512), 512)].astype(F32)
        return total + jnp.sum(part_x * part_x, axis=1, keepdims=True)

    total = lax.fori_loop(0, width // 512, add_square, jnp.zeros((tokens, 1), F32))
    inverse = lax.rsqrt(total / width + EPSILON)
    inv[...] = inverse
    cs[...] = (inverse * cv[...].astype(F32)).astype(BF16)
    send_c.start()

    def term(owner, j, k):
        mine = dot(xv[:, cols(owner, k)], cs[...], 0, 0)
        theirs = dot(xs[j, :, part(k)], css[...], 0, 0)
        return scale * (mine + theirs)

    def keep(k):
        at = part(k)
        mv[at] = MOMENTUM_BETA * mv[at] + WEIGHT_DECAY * pv[at] + term(f, 0, k)

    def product(owner, k):
        piece = w[owner, part(k)]
        fwd[...] += dot(xv[:, cols(owner, k)], piece, 1, 0)
        back[:, cols(owner, k)] = dot(cv[...], piece, 1, 1)

    fwd[...] = jnp.zeros_like(fwd)

    def near(k):
        product(f, k)
        gather_own(k).wait_recv()
        product(f1, k)

    def pass_on(k):
        gather_y(k).wait_recv()
        gather_fwd(k).start()
        if relay:
            swap_p(k).start()

    def far(k):
        product(f2, k)
        gather_fwd(k).wait_recv()
        product(f3, k)

    def fold(k):
        at = part(k)
        send_g(k).wait_recv()
        mid = mv[at] + gr[at].astype(F32)
        mv[at] = mid
        ms[at] = mid.astype(BF16)
        swap_m(k).start()

    send_x(1, f3).wait_recv()
    send_c.wait_recv()
    send_x(0, f1).wait_recv()
    load_m.wait()

    def reduce_step(k):
        gs[part(k)] = term(f2, 1, k).astype(BF16)

        @pl.when(k < depth)
        def _():
            gather_y(early - depth + k).wait_send()

        @pl.when(k >= depth)
        def _():
            send_g(k - depth).wait_send()

        send_g(k).start()

        @pl.when(k < early)
        def _():
            pass_on(k)

        keep(k)
        near(k)

        @pl.when((k >= 1) & (k <= early))
        def _():
            far(k - 1)

        @pl.when(k >= depth)
        def _():
            fold(k - depth)

    loop(0, n, reduce_step)

    def gather_step(k):
        j = k - early

        @pl.when(j < depth)
        def _():
            send_g(n - depth + j).wait_send()

        @pl.when((j >= depth) & (k < n))
        def _():
            gather_y(k - depth).wait_send()

        @pl.when(k < n)
        def _():
            gather_y(k).start()

        @pl.when(j < depth)
        def _():
            fold(n - depth + j)

        @pl.when((j >= 2) & (k < n + 2))
        def _():
            pass_on(k - 2)

        @pl.when(j >= 3)
        def _():
            far(k - 3)

    def drain_first(k):
        gather_own(k).wait_send()
        swap_p(k).wait_recv()
        swap_p(k).wait_send()

    def drain_last(k):
        gather_fwd(k).wait_send()
        swap_m(k).wait()

    loop(early, n + 1, gather_step)
    send_x(0, f1).wait_send()
    send_x(1, f3).wait_send()
    send_c.wait_send()
    if not relay:
        loop(0, n, drain_first)
    loop(n + 1, n + 3, gather_step)
    if relay:
        loop(0, n, drain_first)
    loop(n - depth, n, lambda k: gather_y(k).wait_send())
    loop(0, n, drain_last)


def place(
    cv, xv, fwd, back, inv, pv, rp, mv, rm, vo, igo, po, mo, values, ig, new_p, new_m, done
):
    copies = []

    def leave(source, target):
        copy = pltpu.make_async_copy(source, target, done.at[len(copies)])
        copy.start()
        copies.append(copy)

    size = pv.shape[0] // PIECES
    for j in range(PIECES):
        at = pl.ds(j * size, size)
        momentum = 0.5 * (mv[at] + rm[at].astype(F32))
        new_m[at] = momentum
        leave(new_m.at[at], mo.at[at])
        new_p[at] = 0.5 * (pv[at] + rp[at].astype(F32)) - LEARN_RATE * momentum
        leave(new_p.at[at], po.at[at])
    tokens, width = xv.shape
    scale = width ** (-0.5)
    inverse = inv[...]
    values[...] = (scale * inverse * fwd[...]).astype(BF16)
    leave(values, vo)
    projection = scale * jnp.sum(fwd[...] * cv[...].astype(F32), axis=1, keepdims=True) / width
    first = scale * inverse
    second = inverse**3 * projection
    size = tokens // PIECES
    for j in range(PIECES):
        at = pl.ds(j * size, size)
        rows = slice(j * size, (j + 1) * size)
        ig[at] = (first[rows] * back[at] - second[rows] * xv[at].astype(F32)).astype(BF16)
        leave(ig.at[at], igo.at[at])
    for copy in copies:
        copy.wait()


def settle(*arrays):
    cv, xv, fwd, back, inv, pv, rp, mv, rm = arrays
    results = (cv, xv, pv, mv)
    return pl.pallas_call(
        place,
        out_shape=tuple(jax.ShapeDtypeStruct(a.shape, a.dtype) for a in results),
        in_specs=[pl.BlockSpec(memory_space=pltpu.VMEM)] * 9,
        out_specs=(pl.BlockSpec(memory_space=pl.ANY),) * 4,
        scratch_shapes=[
            pltpu.VMEM(cv.shape, BF16),
            pltpu.VMEM(xv.shape, BF16),
            pltpu.VMEM(pv.shape, F32),
            pltpu.VMEM(mv.shape, F32),
            pltpu.SemaphoreType.DMA((1 + 3 * PIECES,)),
        ],
        compiler_params=pltpu.CompilerParams(vmem_limit_bytes=28 * 2**20),
        name="settle",
    )(*arrays)


def run(level, levels, x, c, p, m):
    tokens, width = x.shape
    rows, units = p.shape
    n = rows // CHUNK
    relay = level == levels - 1
    early, depth = (n // 2, n // 2) if relay else (n // 4, n // 4)
    dma = pltpu.SemaphoreType.DMA
    vmem = pltpu.VMEM
    shape = jax.ShapeDtypeStruct
    outs = pl.pallas_call(
        functools.partial(kernel, 2**level, early, depth, relay),
        out_shape=(
            shape((tokens, units), BF16),
            shape((tokens, width), BF16),
            shape((tokens, units), F32),
            shape((tokens, width), F32),
            shape((tokens, 1), F32),
            shape((rows, units), F32),
            shape((rows, units), BF16),
            shape((rows, units), F32),
            shape((rows, units), BF16),
        ),
        in_specs=[pl.BlockSpec(memory_space=pl.ANY)] * 4,
        out_specs=(pl.BlockSpec(memory_space=vmem),) * 9,
        scratch_shapes=[
            vmem((2, tokens, rows), BF16),
            vmem((tokens, units), BF16),
            vmem((tokens, units), BF16),
            vmem((4, rows, units), BF16),
            vmem((rows, units), BF16),
            vmem((rows, units), BF16),
            vmem((rows, units), BF16),
            dma((n,)), dma, dma, dma,
            dma((2,)), dma((2,)), dma, dma,
            dma((n,)), dma((n,)), dma((n,)), dma((n,)), dma((n,)), dma((n,)),
            dma((n,)), dma((n,)), dma((n,)), dma((n,)), dma((n,)), dma((n,)),
        ],
        compiler_params=pltpu.CompilerParams(
            collective_id=level, has_side_effects=True, vmem_limit_bytes=30 * 2**20
        ),
        name="window" + str(level),
    )(x, c, p, m)
    return settle(*outs)


def on_device(inputs, cotangent, param, momentum, step):
    levels = lax.axis_size("rep").bit_length() - 1
    level = lax.rem(step, levels)
    outs = lax.switch(
        level,
        [functools.partial(run, position, levels) for position in range(levels)],
        inputs[0], cotangent[0], param[0], momentum[0],
    )
    return tuple(out[None] for out in outs)


def solution(mesh):
    placed = P("rep", "fsdp", None)
    return jax.shard_map(
        on_device,
        mesh=mesh,
        in_specs=(placed, placed, placed, placed, P()),
        out_specs=(placed,) * 4,
        check_vma=False,
    )
```
